32 devices in a mesh: rep: 4 (over y, core), fsdp: 8 (over z, x).
Axes of the slice: x: 2, y: 2, z: 4, core: 2. Of those that a mesh axis runs over, the one named last changes fastest.
Arguments:
- tokens: bfloat16 [8192, 8192], P(('rep', 'fsdp')), may hold values from -6 to 6
- cotangent: bfloat16 [8192, 512], P(('rep', 'fsdp')), may hold values from -0.29882812 to 0.29882812
- anchor: float32 [8192, 512], P('fsdp'), may hold values from -0.0625 to 0.0625
- momentum: float32 [8192, 512], P('fsdp'), may hold values from -0.02 to 0.02
- first_moment: float32 [4, 8192, 512], P('rep', 'fsdp'), may hold values from -2 to 2
- second_moment: float32 [4, 8192, 512], P('rep', 'fsdp'), may hold values from 0.05 to 1
- inner_offset: float32 [4, 8192, 512], P('rep', 'fsdp'), may hold values from -0.03 to 0.03
Outputs:
- keys: bfloat16 [8192, 512], P(('rep', 'fsdp'))
- first_new: float32 [4, 8192, 512], P('rep', 'fsdp')
- second_new: float32 [4, 8192, 512], P('rep', 'fsdp')
The draws below stay inside these ranges and needn't reach their ends.
All inputs are finite; a program needn't handle non-finite values.
Results may differ from the reference program's by a relative error of at most 0.005.
Values may be sent and summed in bfloat16 or wider, within the bound.
A program may use at most 128 MiB of HBM per device.

```python
import math
import jax
import jax.numpy as jnp
from jax import lax

D = 8192
TOK_DEV = 256
KH = 512
TOKENS = 8192
N_REP = 4
N_FSDP = 8


def raised(result, key, source, target, parts, factor):
    def block_of(axis_at):
        return (jnp.arange(result.shape[axis_at]) // (result.shape[axis_at] // parts)).reshape((-1,) + (1,) * (result.ndim - 1 - axis_at))

    near = jax.random.permutation(key, parts)[block_of(target)]
    second = (block_of(target) + parts // 2) % parts
    return jnp.where((block_of(source) == near) | (block_of(source) == second), factor * result, result)


def level_of(stream_key, shape, shards, least, largest):
    level, own = 1.0, jax.random.fold_in(stream_key, 6)
    for position, blocks in shards:
        steps = jnp.exp(jax.random.uniform(jax.random.fold_in(own, position), (blocks,), jnp.float32, least / len(shards), largest / len(shards)))
        level = level * jnp.repeat(steps, shape[position] // blocks).reshape([-1 if axis == position else 1 for axis in range(len(shape))])
    return level


def normal_values(own_key, dims, spread, most, cuts=(), kind=jnp.bfloat16):
    result = spread * jax.random.normal(own_key, dims, jnp.float32)
    if cuts:
        result = result * level_of(own_key, dims, cuts, -0.22, 0.18)
    return jnp.clip(result, -most, most).astype(kind)


def heavy_noise(own_key, shape, deviation, bound, pieces, heavy, held_as=jnp.bfloat16):
    values = deviation * jax.random.normal(own_key, shape, jnp.float32)
    if pieces:
        values = values * level_of(own_key, shape, pieces, -0.22, 0.18)
    return jnp.clip(raised(values, jax.random.fold_in(own_key, 3), *heavy), -bound, bound).astype(held_as)


def setup_inputs(seed: int = 0) -> dict:
    seeds = jax.random.split(jax.random.key(seed), 8)
    tokens = heavy_noise(seeds[0], (TOKENS, D), 1.0, 6.0, ((0, 32),), (0, 1, 32, 2.75))
    cotangent = normal_values(seeds[1], (TOKENS, KH), 0.04, 0.29882812, ((0, 32),))
    anchor = normal_values(seeds[2], (D, KH), D ** -0.5, 0.0625, ((0, 8),), jnp.float32)
    momentum = normal_values(seeds[3], (D, KH), 0.003, 0.02, ((0, 8),), jnp.float32)
    first_moment = normal_values(seeds[4], (N_REP, D, KH), 0.3, 2.0, ((0, 4), (1, 8)), jnp.float32)
    second_moment = jnp.clip(jnp.exp(math.log(1.0) - 2.9957323 * jax.random.uniform(seeds[5], (N_REP, D, KH), jnp.float32) ** level_of(seeds[5], (N_REP, D, KH), ((0, 4), (1, 8)), -0.2, 0.2)), 0.05, 1.0)
    inner_offset = normal_values(seeds[6], (N_REP, D, KH), 0.005, 0.03, ((0, 4), (1, 8)), jnp.float32)
    return dict(tokens=tokens, cotangent=cotangent, anchor=anchor, momentum=momentum, first_moment=first_moment, second_moment=second_moment, inner_offset=inner_offset)


def reference(tokens, cotangent, anchor, momentum, first_moment, second_moment, inner_offset):
    group = TOK_DEV * N_FSDP
    grads = []
    for index in range(N_REP):
        xs = tokens[index * group:(index + 1) * group]
        ds = cotangent[index * group:(index + 1) * group]
        grads.append(lax.dot_general(xs, ds, (((0,), (0,)), ((), ())), preferred_element_type=jnp.float32))
    grad = jnp.stack(grads)
    first_new = 0.9 * first_moment + 0.1 * grad
    second_new = 0.95 * second_moment + 0.05 * grad * grad
    current = anchor[None] + inner_offset
    inner = current - 0.001 * (first_new / (jnp.sqrt(second_new) + 1e-08) + 0.1 * current)
    pseudo = lax.optimization_barrier(jnp.sum(anchor[None] - inner, axis=0)) / N_REP
    momentum_new = 0.9 * momentum + pseudo
    anchor_new = anchor - 0.7 * (pseudo + 0.9 * momentum_new)
    weights = anchor_new.astype(jnp.bfloat16)
    keys = jnp.dot(tokens, weights, preferred_element_type=jnp.float32).astype(jnp.bfloat16)
    return (keys, first_new, second_new)
```

```python
import functools
import jax
import jax.numpy as jnp
from jax import lax
from jax.experimental import pallas as pl
from jax.experimental.pallas import tpu as pltpu
from jax.sharding import PartitionSpec as P

VMEM = pl.BlockSpec(memory_space=pltpu.VMEM)


def remote(src, dst, send_sem, recv_sem, rep, fsdp):
    return pltpu.make_async_remote_copy(
        src_ref=src,
        dst_ref=dst,
        send_sem=send_sem,
        recv_sem=recv_sem,
        device_id=(rep, fsdp),
        device_id_type=pl.DeviceIdType.MESH,
    )


def greet(rep, fsdp):
    pl.semaphore_signal(
        pltpu.get_barrier_semaphore(),
        inc=1,
        device_id=(rep, fsdp),
        device_id_type=pl.DeviceIdType.MESH,
    )


def contract_rows(left, right):
    return lax.dot_general(
        left, right, (((0,), (0,)), ((), ())), preferred_element_type=jnp.float32
    )


def grad_kernel(
    n, tokens, cot, grad, tok_p, cot_p, part, recv,
    cot_send, cot_recv, tok_send, tok_recv, part_send, part_recv,
):
    outer = n // 2
    rows = grad.shape[0]
    tile = min(rows, 256)
    r, f = lax.axis_index("rep"), lax.axis_index("fsdp")
    o, b = f // 2, f % 2
    partner = 2 * o + 1 - b

    greet(r, partner)

    @pl.loop(1, outer)
    def _(k):
        greet(r, 2 * ((o + k) % outer) + b)

    pl.semaphore_wait(pltpu.get_barrier_semaphore(), outer)

    def cot_copy():
        return remote(cot, cot_p, cot_send, cot_recv, r, partner)

    def tok_copy(k):
        col = pl.multiple_of((2 * ((o + k) % outer) + 1 - b) * rows, rows)
        return remote(
            tokens.at[:, pl.ds(col, rows)], tok_p.at[k],
            tok_send.at[k], tok_recv.at[k], r, partner,
        )

    def part_copy(k):
        return remote(
            part.at[k], recv.at[k], part_send.at[k], part_recv.at[k],
            r, 2 * ((o + k) % outer) + b,
        )

    def partial(k, j):
        first = pl.multiple_of(j * tile, tile)
        col = pl.multiple_of((2 * ((o + k) % outer) + b) * rows + first, tile)
        return contract_rows(tokens[:, pl.ds(col, tile)], cot[...]) + contract_rows(
            tok_p[k, :, pl.ds(first, tile)], cot_p[...]
        )

    cot_copy().start()

    @pl.loop(1, outer)
    def _(k):
        tok_copy(k).start()

    tok_copy(0).start()
    cot_copy().wait_recv()

    @pl.loop(1, outer)
    def _(k):
        tok_copy(k).wait_recv()

        @pl.loop(0, rows // tile)
        def _(j):
            at = pl.ds(pl.multiple_of(j * tile, tile), tile)
            part[k, at, :] = partial(k, j).astype(part.dtype)

        part_copy(k).start()

    tok_copy(0).wait_recv()

    @pl.loop(0, rows // tile)
    def _(j):
        grad[pl.ds(pl.multiple_of(j * tile, tile), tile), :] = partial(0, j)

    @pl.loop(1, outer)
    def _(k):
        part_copy(k).wait_recv()

        @pl.loop(0, rows // tile)
        def _(j):
            at = pl.ds(pl.multiple_of(j * tile, tile), tile)
            grad[at, :] += recv[k, at, :].astype(jnp.float32)

    cot_copy().wait_send()
    tok_copy(0).wait_send()

    @pl.loop(1, outer)
    def _(k):
        tok_copy(k).wait_send()
        part_copy(k).wait_send()


def group_grad(mesh, tokens, cotangent):
    n = mesh.shape["fsdp"]
    outer = n // 2
    count, width = tokens.shape
    kh = cotangent.shape[1]
    rows = width // n
    dma = pltpu.SemaphoreType.DMA
    return pl.pallas_call(
        functools.partial(grad_kernel, n),
        out_shape=jax.ShapeDtypeStruct((rows, kh), jnp.float32),
        in_specs=[VMEM] * 2,
        out_specs=VMEM,
        scratch_shapes=[
            pltpu.VMEM((outer, count, rows), jnp.bfloat16),
            pltpu.VMEM((count, kh), jnp.bfloat16),
            pltpu.VMEM((outer, rows, kh), jnp.bfloat16),
            pltpu.VMEM((outer, rows, kh), jnp.bfloat16),
            dma, dma, dma((outer,)), dma((outer,)), dma((outer,)), dma((outer,)),
        ],
        compiler_params=pltpu.CompilerParams(
            collective_id=0, has_side_effects=True, vmem_limit_bytes=40 * 2**20
        ),
    )(tokens, cotangent)


def keys_kernel(
    n, tokens, delta, anchor, momentum, keys, got, weights, total,
    got_send, got_recv, z_send, z_recv, x_send, x_recv,
    y_send, y_recv, c_send, c_recv, d_send, d_recv,
):
    outer = n // 2
    rows = anchor.shape[0]
    quarter = rows // 4
    r, f = lax.axis_index("rep"), lax.axis_index("fsdp")
    o, b = f // 2, f % 2
    partner = 2 * o + 1 - b
    over, near = (r + 2) % 4, r + 1 - 2 * (r % 2)

    greet(r, partner)

    @pl.loop(1, outer)
    def _(k):
        greet(r, 2 * ((o + k) % outer) + b)

    for m in range(1, 4):
        greet((r + m) % 4, f)
    pl.semaphore_wait(pltpu.get_barrier_semaphore(), outer + 3)

    def quarter_of(rep):
        return pl.ds(pl.multiple_of(rep * quarter, quarter), quarter)

    def chunk(fsdp, rep):
        return weights.at[pl.ds(pl.multiple_of(fsdp * rows + rep * quarter, quarter), quarter)]

    def got_copy(m):
        to = (r + m) % 4
        return remote(
            delta.at[quarter_of(to)], got.at[m - 1],
            got_send.at[m - 1], got_recv.at[m - 1], to, f,
        )

    for m in (2, 1, 3):
        got_copy(m).start()
    mine = quarter_of(r)
    for m in (1, 2, 3):
        got_copy(m).wait_recv()
    pseudo = (
        (delta[mine, :].astype(jnp.float32) + got[0].astype(jnp.float32))
        + (got[1].astype(jnp.float32) + got[2].astype(jnp.float32))
    ) / 4
    momentum_new = 0.9 * momentum[mine, :] + pseudo
    anchor_new = anchor[mine, :] - 0.7 * (pseudo + 0.9 * momentum_new)
    own = pl.ds(pl.multiple_of(f * rows + r * quarter, quarter), quarter)
    weights[own, :] = anchor_new.astype(weights.dtype)

    def z_copy(k):
        ref = chunk(f, r)
        return remote(ref, ref, z_send.at[k], z_recv.at[k], r, 2 * ((o + k) % outer) + b)

    def source(k, parity):
        return 2 * ((o + outer - k) % outer) + parity

    def x_copy(k):
        ref = chunk(source(k, b), r)
        return remote(ref, ref, x_send.at[k], x_recv.at[k], r, partner)

    def y_copy(k, s):
        ref = chunk(source(k, b if s == 0 else 1 - b), r)
        return remote(ref, ref, y_send.at[k, s], y_recv.at[k, s], over, f)

    def c_copy(k, s):
        ref = chunk(source(k, b if s == 0 else 1 - b), r)
        return remote(ref, ref, c_send.at[k, s], c_recv.at[k, s], near, f)

    def d_copy(k, s):
        ref = chunk(source(k, b if s == 0 else 1 - b), over)
        return remote(ref, ref, d_send.at[k, s], d_recv.at[k, s], near, f)

    @pl.loop(1, outer)
    def _(k):
        z_copy(k).start()

    total[...] = jnp.zeros_like(total)

    @pl.loop(0, outer + 3)
    def _(i):
        @pl.when(i < outer)
        def _():
            @pl.when(i > 0)
            def _():
                z_copy(i).wait_recv()

            x_copy(i).start()
            y_copy(i, 0).start()
            c_copy(i, 0).start()

        @pl.when((i >= 1) & (i < outer + 1))
        def _():
            x_copy(i - 1).wait_recv()
            y_copy(i - 1, 1).start()
            c_copy(i - 1, 1).start()

        @pl.when((i >= 2) & (i < outer + 2))
        def _():
            for s in range(2):
                y_copy(i - 2, s).wait_recv()
                d_copy(i - 2, s).start()

        @pl.when(i >= 3)
        def _():
            k = i - 3
            for s in range(2):
                c_copy(k, s).wait_recv()
                d_copy(k, s).wait_recv()
            at = pl.ds(pl.multiple_of(source(k, 0) * rows, 2 * rows), 2 * rows)
            total[...] += jnp.dot(
                tokens[:, at], weights[at, :], preferred_element_type=jnp.float32
            )

    keys[...] = total[...].astype(keys.dtype)
    for m in (1, 2, 3):
        got_copy(m).wait_send()

    @pl.loop(0, outer)
    def _(k):
        @pl.when(k > 0)
        def _():
            z_copy(k).wait_send()

        x_copy(k).wait_send()
        for s in range(2):
            y_copy(k, s).wait_send()
            c_copy(k, s).wait_send()
            d_copy(k, s).wait_send()


def keys_of(mesh, tokens, delta, anchor, momentum):
    n = mesh.shape["fsdp"]
    outer = n // 2
    count, width = tokens.shape
    rows, kh = anchor.shape
    dma = pltpu.SemaphoreType.DMA
    return pl.pallas_call(
        functools.partial(keys_kernel, n),
        out_shape=jax.ShapeDtypeStruct((count, kh), jnp.bfloat16),
        in_specs=[VMEM] * 4,
        out_specs=VMEM,
        scratch_shapes=[
            pltpu.VMEM((3, rows // 4, kh), jnp.bfloat16),
            pltpu.VMEM((width, kh), jnp.bfloat16),
            pltpu.VMEM((count, kh), jnp.float32),
            dma((3,)), dma((3,)),
            dma((outer,)), dma((outer,)), dma((outer,)), dma((outer,)),
            dma((outer, 2)), dma((outer, 2)), dma((outer, 2)), dma((outer, 2)),
            dma((outer, 2)), dma((outer, 2)),
        ],
        compiler_params=pltpu.CompilerParams(
            collective_id=1, has_side_effects=True, vmem_limit_bytes=40 * 2**20
        ),
    )(tokens, delta, anchor, momentum)


def on_device(mesh, tokens, cotangent, anchor, momentum, first_moment, second_moment, inner_offset):
    grad = group_grad(mesh, tokens, cotangent)[None]
    first_new = 0.9 * first_moment + 0.1 * grad
    second_new = 0.95 * second_moment + 0.05 * grad * grad
    current = anchor[None] + inner_offset
    inner = current - 0.001 * (first_new / (jnp.sqrt(second_new) + 1e-08) + 0.1 * current)
    delta = (anchor - inner[0]).astype(jnp.bfloat16)
    keys = keys_of(mesh, tokens, delta, anchor, momentum)
    return (keys, first_new, second_new)


def solution(mesh):
    return jax.shard_map(
        functools.partial(on_device, mesh),
        mesh=mesh,
        in_specs=(
            P(("rep", "fsdp"), None),
            P(("rep", "fsdp"), None),
            P("fsdp", None),
            P("fsdp", None),
            P("rep", "fsdp", None),
            P("rep", "fsdp", None),
            P("rep", "fsdp", None),
        ),
        out_specs=(P(("rep", "fsdp"), None), P("rep", "fsdp", None), P("rep", "fsdp", None)),
        check_vma=False,
    )
```

```python
import functools
import jax
import jax.numpy as jnp
from jax import lax
from jax.experimental import pallas as pl
from jax.experimental.pallas import tpu as pltpu
from jax.sharding import PartitionSpec as P

VMEM = pl.BlockSpec(memory_space=pltpu.VMEM)


def remote(src, dst, send_sem, recv_sem, rep, fsdp):
    return pltpu.make_async_remote_copy(
        src_ref=src,
        dst_ref=dst,
        send_sem=send_sem,
        recv_sem=recv_sem,
        device_id=(rep, fsdp),
        device_id_type=pl.DeviceIdType.MESH,
    )


def greet(rep, fsdp):
    pl.semaphore_signal(
        pltpu.get_barrier_semaphore(),
        inc=1,
        device_id=(rep, fsdp),
        device_id_type=pl.DeviceIdType.MESH,
    )


def contract_rows(left, right):
    return lax.dot_general(
        left, right, (((0,), (0,)), ((), ())), preferred_element_type=jnp.float32
    )


def grad_kernel(
    n, tokens, cot, grad, tok_p, cot_p, part, recv,
    cot_send, cot_recv, tok_send, tok_recv, part_send, part_recv,
):
    outer = n // 2
    rows = grad.shape[0]
    tile = min(rows, 256)
    r, f = lax.axis_index("rep"), lax.axis_index("fsdp")
    o, b = f // 2, f % 2
    partner = 2 * o + 1 - b

    greet(r, partner)

    @pl.loop(1, outer)
    def _(k):
        greet(r, 2 * ((o + k) % outer) + b)

    pl.semaphore_wait(pltpu.get_barrier_semaphore(), outer)

    def cot_copy():
        return remote(cot, cot_p, cot_send, cot_recv, r, partner)

    def tok_copy(k):
        col = pl.multiple_of((2 * ((o + k) % outer) + 1 - b) * rows, rows)
        return remote(
            tokens.at[:, pl.ds(col, rows)], tok_p.at[k],
            tok_send.at[k], tok_recv.at[k], r, partner,
        )

    def part_copy(k):
        return remote(
            part.at[k], recv.at[k], part_send.at[k], part_recv.at[k],
            r, 2 * ((o + k) % outer) + b,
        )

    def partial(k, j):
        first = pl.multiple_of(j * tile, tile)
        col = pl.multiple_of((2 * ((o + k) % outer) + b) * rows + first, tile)
        return contract_rows(tokens[:, pl.ds(col, tile)], cot[...]) + contract_rows(
            tok_p[k, :, pl.ds(first, tile)], cot_p[...]
        )

    cot_copy().start()

    @pl.loop(1, outer)
    def _(k):
        tok_copy(k).start()

    tok_copy(0).start()
    cot_copy().wait_recv()

    @pl.loop(1, outer)
    def _(k):
        tok_copy(k).wait_recv()

        @pl.loop(0, rows // tile)
        def _(j):
            at = pl.ds(pl.multiple_of(j * tile, tile), tile)
            part[k, at, :] = partial(k, j).astype(part.dtype)

        part_copy(k).start()

    tok_copy(0).wait_recv()

    @pl.loop(0, rows // tile)
    def _(j):
        grad[pl.ds(pl.multiple_of(j * tile, tile), tile), :] = partial(0, j)

    @pl.loop(1, outer)
    def _(k):
        part_copy(k).wait_recv()

        @pl.loop(0, rows // tile)
        def _(j):
            at = pl.ds(pl.multiple_of(j * tile, tile), tile)
            grad[at, :] += recv[k, at, :].astype(jnp.float32)

    cot_copy().wait_send()
    tok_copy(0).wait_send()

    @pl.loop(1, outer)
    def _(k):
        tok_copy(k).wait_send()
        part_copy(k).wait_send()


HALVES = 2


def line_kernel(
    tokens, cot, grad, tok_p, cot_p, part, recv,
    cot_send, cot_recv, tok_send, tok_recv, part_send, part_recv,
):
    rows = grad.shape[0]
    half = rows // HALVES
    tile = min(half, 256)
    r, f = lax.axis_index("rep"), lax.axis_index("fsdp")
    o, b = f // 2, f % 2
    partner = 2 * o + 1 - b
    side = o // 2
    inner = (o + side) % 2

    def pair(q):
        return q + side * (3 - 2 * q)

    greet(r, partner)
    for k in range(1, 4):
        greet(r, 2 * ((o + k) % 4) + b)
    pl.semaphore_wait(pltpu.get_barrier_semaphore(), 4)

    def block(i):
        return (3 + inner - i) % 4

    def cot_copy():
        return remote(cot, cot_p, cot_send, cot_recv, r, partner)

    def tok_copy(i, h):
        col = pl.multiple_of((2 * pair(block(i)) + 1 - b) * rows + h * half, half)
        return remote(
            tokens.at[:, pl.ds(col, half)], tok_p.at[i, h],
            tok_send.at[i, h], tok_recv.at[i, h], r, partner,
        )

    def part_copy(i, h):
        slot = i + inner * (2, 2, 1)[i]
        to = pair(inner * block(i) + 1 - inner)
        return remote(
            part.at[i, h], recv.at[slot, h], part_send.at[i, h], part_recv.at[slot, h],
            r, 2 * to + b,
        )

    def received(slot, h):
        return remote(
            part.at[0, h], recv.at[slot, h], part_send.at[0, h], part_recv.at[slot, h],
            r, partner,
        )

    def partial(i, h, j):
        first = pl.multiple_of(j * tile, tile)
        col = pl.multiple_of((2 * pair(block(i)) + b) * rows + h * half + first, tile)
        return contract_rows(tokens[:, pl.ds(col, tile)], cot[...]) + contract_rows(
            tok_p[i, h, :, pl.ds(first, tile)], cot_p[...]
        )

    cot_copy().start()
    for i in range(4):
        for h in range(HALVES):
            tok_copy(i, h).start()
    cot_copy().wait_recv()
    for i in range(3):
        for h in range(HALVES):
            tok_copy(i, h).wait_recv()

            @pl.when((inner == 0) | (i == 0))
            def _():
                @pl.loop(0, half // tile)
                def _(j):
                    at = pl.ds(pl.multiple_of(j * tile, tile), tile)
                    part[i, h, at, :] = partial(i, h, j).astype(part.dtype)

            if i > 0:
                @pl.when(inner == 1)
                def _():
                    received(i - 1, h).wait_recv()

                    @pl.loop(0, half // tile)
                    def _(j):
                        at = pl.ds(pl.multiple_of(j * tile, tile), tile)
                        total = partial(i, h, j) + recv[i - 1, h, at, :].astype(jnp.float32)
                        part[i, h, at, :] = total.astype(part.dtype)

            part_copy(i, h).start()

    for h in range(HALVES):
        tok_copy(3, h).wait_recv()

        @pl.loop(0, half // tile)
        def _(j):
            at = pl.ds(pl.multiple_of(h * half + j * tile, tile), tile)
            grad[at, :] = partial(3, h, j)

    for h in range(HALVES):
        for slot in (2, 3):
            received(slot, h).wait_recv()

            @pl.loop(0, half // tile)
            def _(j):
                at = pl.ds(pl.multiple_of(h * half + j * tile, tile), tile)
                there = pl.ds(pl.multiple_of(j * tile, tile), tile)
                grad[at, :] += recv[slot, h, there, :].astype(jnp.float32)

    cot_copy().wait_send()
    for h in range(HALVES):
        for i in range(4):
            tok_copy(i, h).wait_send()
        for i in range(3):
            part_copy(i, h).wait_send()


def line_grad(tokens, cotangent):
    count, width = tokens.shape
    kh = cotangent.shape[1]
    rows = width // 8
    half = rows // HALVES
    dma = pltpu.SemaphoreType.DMA
    return pl.pallas_call(
        line_kernel,
        out_shape=jax.ShapeDtypeStruct((rows, kh), jnp.float32),
        in_specs=[VMEM] * 2,
        out_specs=VMEM,
        scratch_shapes=[
            pltpu.VMEM((4, HALVES, count, half), jnp.bfloat16),
            pltpu.VMEM((count, kh), jnp.bfloat16),
            pltpu.VMEM((3, HALVES, half, kh), jnp.bfloat16),
            pltpu.VMEM((4, HALVES, half, kh), jnp.bfloat16),
            dma, dma, dma((4, HALVES)), dma((4, HALVES)), dma((3, HALVES)), dma((4, HALVES)),
        ],
        compiler_params=pltpu.CompilerParams(
            collective_id=0, has_side_effects=True, vmem_limit_bytes=40 * 2**20
        ),
    )(tokens, cotangent)


def group_grad(mesh, tokens, cotangent):
    n = mesh.shape["fsdp"]
    if n == 8:
        return line_grad(tokens, cotangent)
    outer = n // 2
    count, width = tokens.shape
    kh = cotangent.shape[1]
    rows = width // n
    dma = pltpu.SemaphoreType.DMA
    return pl.pallas_call(
        functools.partial(grad_kernel, n),
        out_shape=jax.ShapeDtypeStruct((rows, kh), jnp.float32),
        in_specs=[VMEM] * 2,
        out_specs=VMEM,
        scratch_shapes=[
            pltpu.VMEM((outer, count, rows), jnp.bfloat16),
            pltpu.VMEM((count, kh), jnp.bfloat16),
            pltpu.VMEM((outer, rows, kh), jnp.bfloat16),
            pltpu.VMEM((outer, rows, kh), jnp.bfloat16),
            dma, dma, dma((outer,)), dma((outer,)), dma((outer,)), dma((outer,)),
        ],
        compiler_params=pltpu.CompilerParams(
            collective_id=0, has_side_effects=True, vmem_limit_bytes=40 * 2**20
        ),
    )(tokens, cotangent)


def keys_kernel(
    n, tokens, delta, anchor, momentum, keys, got, weights, total,
    got_send, got_recv, z_send, z_recv, x_send, x_recv,
    y_send, y_recv, c_send, c_recv, d_send, d_recv,
):
    outer = n // 2
    rows = anchor.shape[0]
    quarter = rows // 4
    r, f = lax.axis_index("rep"), lax.axis_index("fsdp")
    o, b = f // 2, f % 2
    partner = 2 * o + 1 - b
    over, near = (r + 2) % 4, r + 1 - 2 * (r % 2)

    greet(r, partner)

    @pl.loop(1, outer)
    def _(k):
        greet(r, 2 * ((o + k) % outer) + b)

    for m in range(1, 4):
        greet((r + m) % 4, f)
    pl.semaphore_wait(pltpu.get_barrier_semaphore(), outer + 3)

    def quarter_of(rep):
        return pl.ds(pl.multiple_of(rep * quarter, quarter), quarter)

    def chunk(fsdp, rep):
        return weights.at[pl.ds(pl.multiple_of(fsdp * rows + rep * quarter, quarter), quarter)]

    def got_copy(m):
        to = (r + m) % 4
        return remote(
            delta.at[quarter_of(to)], got.at[m - 1],
            got_send.at[m - 1], got_recv.at[m - 1], to, f,
        )

    for m in (2, 1, 3):
        got_copy(m).start()
    mine = quarter_of(r)
    for m in (1, 2, 3):
        got_copy(m).wait_recv()
    pseudo = (
        (delta[mine, :].astype(jnp.float32) + got[0].astype(jnp.float32))
        + (got[1].astype(jnp.float32) + got[2].astype(jnp.float32))
    ) / 4
    momentum_new = 0.9 * momentum[mine, :] + pseudo
    anchor_new = anchor[mine, :] - 0.7 * (pseudo + 0.9 * momentum_new)
    own = pl.ds(pl.multiple_of(f * rows + r * quarter, quarter), quarter)
    weights[own, :] = anchor_new.astype(weights.dtype)

    def z_copy(k):
        ref = chunk(f, r)
        return remote(ref, ref, z_send.at[k], z_recv.at[k], r, 2 * ((o + k) % outer) + b)

    def source(k, parity):
        return 2 * ((o + outer - k) % outer) + parity

    def x_copy(k):
        ref = chunk(source(k, b), r)
        return remote(ref, ref, x_send.at[k], x_recv.at[k], r, partner)

    def y_copy(k, s):
        ref = chunk(source(k, b if s == 0 else 1 - b), r)
        return remote(ref, ref, y_send.at[k, s], y_recv.at[k, s], over, f)

    def c_copy(k, s):
        ref = chunk(source(k, b if s == 0 else 1 - b), r)
        return remote(ref, ref, c_send.at[k, s], c_recv.at[k, s], near, f)

    def d_copy(k, s):
        ref = chunk(source(k, b if s == 0 else 1 - b), over)
        return remote(ref, ref, d_send.at[k, s], d_recv.at[k, s], near, f)

    @pl.loop(1, outer)
    def _(k):
        z_copy(k).start()

    total[...] = jnp.zeros_like(total)

    @pl.loop(0, outer + 3)
    def _(i):
        @pl.when(i < outer)
        def _():
            @pl.when(i > 0)
            def _():
                z_copy(i).wait_recv()

            x_copy(i).start()
            y_copy(i, 0).start()
            c_copy(i, 0).start()

        @pl.when((i >= 1) & (i < outer + 1))
        def _():
            x_copy(i - 1).wait_recv()
            y_copy(i - 1, 1).start()
            c_copy(i - 1, 1).start()

        @pl.when((i >= 2) & (i < outer + 2))
        def _():
            for s in range(2):
                y_copy(i - 2, s).wait_recv()
                d_copy(i - 2, s).start()

        @pl.when(i >= 3)
        def _():
            k = i - 3
            for s in range(2):
                c_copy(k, s).wait_recv()
                d_copy(k, s).wait_recv()
            at = pl.ds(pl.multiple_of(source(k, 0) * rows, 2 * rows), 2 * rows)
            total[...] += jnp.dot(
                tokens[:, at], weights[at, :], preferred_element_type=jnp.float32
            )

    keys[...] = total[...].astype(keys.dtype)
    for m in (1, 2, 3):
        got_copy(m).wait_send()

    @pl.loop(0, outer)
    def _(k):
        @pl.when(k > 0)
        def _():
            z_copy(k).wait_send()

        x_copy(k).wait_send()
        for s in range(2):
            y_copy(k, s).wait_send()
            c_copy(k, s).wait_send()
            d_copy(k, s).wait_send()


def keys_of(mesh, tokens, delta, anchor, momentum):
    n = mesh.shape["fsdp"]
    outer = n // 2
    count, width = tokens.shape
    rows, kh = anchor.shape
    dma = pltpu.SemaphoreType.DMA
    return pl.pallas_call(
        functools.partial(keys_kernel, n),
        out_shape=jax.ShapeDtypeStruct((count, kh), jnp.bfloat16),
        in_specs=[VMEM] * 4,
        out_specs=VMEM,
        scratch_shapes=[
            pltpu.VMEM((3, rows // 4, kh), jnp.bfloat16),
            pltpu.VMEM((width, kh), jnp.bfloat16),
            pltpu.VMEM((count, kh), jnp.float32),
            dma((3,)), dma((3,)),
            dma((outer,)), dma((outer,)), dma((outer,)), dma((outer,)),
            dma((outer, 2)), dma((outer, 2)), dma((outer, 2)), dma((outer, 2)),
            dma((outer, 2)), dma((outer, 2)),
        ],
        compiler_params=pltpu.CompilerParams(
            collective_id=1, has_side_effects=True, vmem_limit_bytes=40 * 2**20
        ),
    )(tokens, delta, anchor, momentum)


def on_device(mesh, tokens, cotangent, anchor, momentum, first_moment, second_moment, inner_offset):
    grad = group_grad(mesh, tokens, cotangent)[None]
    first_new = 0.9 * first_moment + 0.1 * grad
    second_new = 0.95 * second_moment + 0.05 * grad * grad
    current = anchor[None] + inner_offset
    inner = current - 0.001 * (first_new / (jnp.sqrt(second_new) + 1e-08) + 0.1 * current)
    delta = (anchor - inner[0]).astype(jnp.bfloat16)
    keys = keys_of(mesh, tokens, delta, anchor, momentum)
    return (keys, first_new, second_new)


def solution(mesh):
    return jax.shard_map(
        functools.partial(on_device, mesh),
        mesh=mesh,
        in_specs=(
            P(("rep", "fsdp"), None),
            P(("rep", "fsdp"), None),
            P("fsdp", None),
            P("fsdp", None),
            P("rep", "fsdp", None),
            P("rep", "fsdp", None),
            P("rep", "fsdp", None),
        ),
        out_specs=(P(("rep", "fsdp"), None), P("rep", "fsdp", None), P("rep", "fsdp", None)),
        check_vma=False,
    )
```

```python
import functools
import jax
import jax.numpy as jnp
from jax import lax
from jax.experimental import pallas as pl
from jax.experimental.pallas import tpu as pltpu
from jax.sharding import PartitionSpec as P

VMEM = pl.BlockSpec(memory_space=pltpu.VMEM)


def remote(src, dst, send_sem, recv_sem, rep, fsdp):
    return pltpu.make_async_remote_copy(
        src_ref=src,
        dst_ref=dst,
        send_sem=send_sem,
        recv_sem=recv_sem,
        device_id=(rep, fsdp),
        device_id_type=pl.DeviceIdType.MESH,
    )


def greet(rep, fsdp):
    pl.semaphore_signal(
        pltpu.get_barrier_semaphore(),
        inc=1,
        device_id=(rep, fsdp),
        device_id_type=pl.DeviceIdType.MESH,
    )


def contract_rows(left, right):
    return lax.dot_general(
        left, right, (((0,), (0,)), ((), ())), preferred_element_type=jnp.float32
    )


def grad_kernel(
    n, tokens, cot, grad, tok_p, cot_p, part, recv,
    cot_send, cot_recv, tok_send, tok_recv, part_send, part_recv,
):
    outer = n // 2
    rows = grad.shape[0]
    tile = min(rows, 256)
    r, f = lax.axis_index("rep"), lax.axis_index("fsdp")
    o, b = f // 2, f % 2
    partner = 2 * o + 1 - b

    greet(r, partner)

    @pl.loop(1, outer)
    def _(k):
        greet(r, 2 * ((o + k) % outer) + b)

    pl.semaphore_wait(pltpu.get_barrier_semaphore(), outer)

    def cot_copy():
        return remote(cot, cot_p, cot_send, cot_recv, r, partner)

    def tok_copy(k):
        col = pl.multiple_of((2 * ((o + k) % outer) + 1 - b) * rows, rows)
        return remote(
            tokens.at[:, pl.ds(col, rows)], tok_p.at[k],
            tok_send.at[k], tok_recv.at[k], r, partner,
        )

    def part_copy(k):
        return remote(
            part.at[k], recv.at[k], part_send.at[k], part_recv.at[k],
            r, 2 * ((o + k) % outer) + b,
        )

    def partial(k, j):
        first = pl.multiple_of(j * tile, tile)
        col = pl.multiple_of((2 * ((o + k) % outer) + b) * rows + first, tile)
        return contract_rows(tokens[:, pl.ds(col, tile)], cot[...]) + contract_rows(
            tok_p[k, :, pl.ds(first, tile)], cot_p[...]
        )

    cot_copy().start()

    @pl.loop(1, outer)
    def _(k):
        tok_copy(k).start()

    tok_copy(0).start()
    cot_copy().wait_recv()

    @pl.loop(1, outer)
    def _(k):
        tok_copy(k).wait_recv()

        @pl.loop(0, rows // tile)
        def _(j):
            at = pl.ds(pl.multiple_of(j * tile, tile), tile)
            part[k, at, :] = partial(k, j).astype(part.dtype)

        part_copy(k).start()

    tok_copy(0).wait_recv()

    @pl.loop(0, rows // tile)
    def _(j):
        grad[pl.ds(pl.multiple_of(j * tile, tile), tile), :] = partial(0, j)

    @pl.loop(1, outer)
    def _(k):
        part_copy(k).wait_recv()

        @pl.loop(0, rows // tile)
        def _(j):
            at = pl.ds(pl.multiple_of(j * tile, tile), tile)
            grad[at, :] += recv[k, at, :].astype(jnp.float32)

    cot_copy().wait_send()
    tok_copy(0).wait_send()

    @pl.loop(1, outer)
    def _(k):
        tok_copy(k).wait_send()
        part_copy(k).wait_send()


HALVES = 2


def line_kernel(
    tokens, cot, grad, tok_p, cot_p, part, recv,
    cot_send, cot_recv, tok_send, tok_recv, part_send, part_recv,
):
    rows = grad.shape[0]
    half = rows // HALVES
    tile = min(half, 256)
    r, f = lax.axis_index("rep"), lax.axis_index("fsdp")
    o, b = f // 2, f % 2
    partner = 2 * o + 1 - b
    side = o // 2
    inner = (o + side) % 2

    def pair(q):
        return q + side * (3 - 2 * q)

    greet(r, partner)
    for k in range(1, 4):
        greet(r, 2 * ((o + k) % 4) + b)
    pl.semaphore_wait(pltpu.get_barrier_semaphore(), 4)

    def block(i):
        return (3 + inner - i) % 4

    def cot_copy():
        return remote(cot, cot_p, cot_send, cot_recv, r, partner)

    def tok_copy(i, h):
        col = pl.multiple_of((2 * pair(block(i)) + 1 - b) * rows + h * half, half)
        return remote(
            tokens.at[:, pl.ds(col, half)], tok_p.at[i, h],
            tok_send.at[i, h], tok_recv.at[i, h], r, partner,
        )

    def part_copy(i, h):
        slot = i + inner * (2, 2, 1)[i]
        to = pair(inner * block(i) + 1 - inner)
        return remote(
            part.at[i, h], recv.at[slot, h], part_send.at[i, h], part_recv.at[slot, h],
            r, 2 * to + b,
        )

    def received(slot, h):
        return remote(
            part.at[0, h], recv.at[slot, h], part_send.at[0, h], part_recv.at[slot, h],
            r, partner,
        )

    def partial(i, h, j):
        first = pl.multiple_of(j * tile, tile)
        col = pl.multiple_of((2 * pair(block(i)) + b) * rows + h * half + first, tile)
        return contract_rows(tokens[:, pl.ds(col, tile)], cot[...]) + contract_rows(
            tok_p[i, h, :, pl.ds(first, tile)], cot_p[...]
        )

    cot_copy().start()
    for i in range(4):
        for h in range(HALVES):
            tok_copy(i, h).start()
    cot_copy().wait_recv()
    for i in range(3):
        for h in range(HALVES):
            tok_copy(i, h).wait_recv()

            @pl.when((inner == 0) | (i == 0))
            def _():
                @pl.loop(0, half // tile)
                def _(j):
                    at = pl.ds(pl.multiple_of(j * tile, tile), tile)
                    part[i, h, at, :] = partial(i, h, j).astype(part.dtype)

            if i > 0:
                @pl.when(inner == 1)
                def _():
                    received(i - 1, h).wait_recv()

                    @pl.loop(0, half // tile)
                    def _(j):
                        at = pl.ds(pl.multiple_of(j * tile, tile), tile)
                        total = partial(i, h, j) + recv[i - 1, h, at, :].astype(jnp.float32)
                        part[i, h, at, :] = total.astype(part.dtype)

            part_copy(i, h).start()

    for h in range(HALVES):
        tok_copy(3, h).wait_recv()

        @pl.loop(0, half // tile)
        def _(j):
            at = pl.ds(pl.multiple_of(h * half + j * tile, tile), tile)
            grad[at, :] = partial(3, h, j)

    for h in range(HALVES):
        for slot in (2, 3):
            received(slot, h).wait_recv()

            @pl.loop(0, half // tile)
            def _(j):
                at = pl.ds(pl.multiple_of(h * half + j * tile, tile), tile)
                there = pl.ds(pl.multiple_of(j * tile, tile), tile)
                grad[at, :] += recv[slot, h, there, :].astype(jnp.float32)

    cot_copy().wait_send()
    for h in range(HALVES):
        for i in range(4):
            tok_copy(i, h).wait_send()
        for i in range(3):
            part_copy(i, h).wait_send()


def line_grad(tokens, cotangent):
    count, width = tokens.shape
    kh = cotangent.shape[1]
    rows = width // 8
    half = rows // HALVES
    dma = pltpu.SemaphoreType.DMA
    return pl.pallas_call(
        line_kernel,
        out_shape=jax.ShapeDtypeStruct((rows, kh), jnp.float32),
        in_specs=[VMEM] * 2,
        out_specs=VMEM,
        scratch_shapes=[
            pltpu.VMEM((4, HALVES, count, half), jnp.bfloat16),
            pltpu.VMEM((count, kh), jnp.bfloat16),
            pltpu.VMEM((3, HALVES, half, kh), jnp.bfloat16),
            pltpu.VMEM((4, HALVES, half, kh), jnp.bfloat16),
            dma, dma, dma((4, HALVES)), dma((4, HALVES)), dma((3, HALVES)), dma((4, HALVES)),
        ],
        compiler_params=pltpu.CompilerParams(
            collective_id=0, has_side_effects=True, vmem_limit_bytes=40 * 2**20
        ),
    )(tokens, cotangent)


def group_grad(mesh, tokens, cotangent):
    n = mesh.shape["fsdp"]
    if n == 8:
        return line_grad(tokens, cotangent)
    outer = n // 2
    count, width = tokens.shape
    kh = cotangent.shape[1]
    rows = width // n
    dma = pltpu.SemaphoreType.DMA
    return pl.pallas_call(
        functools.partial(grad_kernel, n),
        out_shape=jax.ShapeDtypeStruct((rows, kh), jnp.float32),
        in_specs=[VMEM] * 2,
        out_specs=VMEM,
        scratch_shapes=[
            pltpu.VMEM((outer, count, rows), jnp.bfloat16),
            pltpu.VMEM((count, kh), jnp.bfloat16),
            pltpu.VMEM((outer, rows, kh), jnp.bfloat16),
            pltpu.VMEM((outer, rows, kh), jnp.bfloat16),
            dma, dma, dma((outer,)), dma((outer,)), dma((outer,)), dma((outer,)),
        ],
        compiler_params=pltpu.CompilerParams(
            collective_id=0, has_side_effects=True, vmem_limit_bytes=40 * 2**20
        ),
    )(tokens, cotangent)


def keys_kernel(
    n, tokens, delta, anchor, momentum, keys, got, weights, total,
    got_send, got_recv, z_send, z_recv, first_send, first_recv,
    second_send, second_recv, near_send, near_recv,
):
    outer = n // 2
    rows = anchor.shape[0]
    quarter = rows // 4
    r, f = lax.axis_index("rep"), lax.axis_index("fsdp")
    o, b = f // 2, f % 2
    partner = 2 * o + 1 - b
    over, near = (r + 2) % 4, r + 1 - 2 * (r % 2)

    greet(r, partner)

    @pl.loop(1, outer)
    def _(k):
        greet(r, 2 * ((o + k) % outer) + b)

    for m in range(1, 4):
        greet((r + m) % 4, f)
    pl.semaphore_wait(pltpu.get_barrier_semaphore(), outer + 3)

    def quarter_of(rep):
        return pl.ds(pl.multiple_of(rep * quarter, quarter), quarter)

    def chunk(fsdp, rep, h):
        at = fsdp * rows + rep * quarter + h * (quarter // 2)
        return weights.at[pl.ds(pl.multiple_of(at, quarter // 2), quarter // 2)]

    def got_copy(m):
        to = (r + m) % 4
        return remote(
            delta.at[quarter_of(to)], got.at[m - 1],
            got_send.at[m - 1], got_recv.at[m - 1], to, f,
        )

    for m in (2, 1, 3):
        got_copy(m).start()
    mine = quarter_of(r)
    for m in (1, 2, 3):
        got_copy(m).wait_recv()
    pseudo = (
        (delta[mine, :].astype(jnp.float32) + got[0].astype(jnp.float32))
        + (got[1].astype(jnp.float32) + got[2].astype(jnp.float32))
    ) / 4
    momentum_new = 0.9 * momentum[mine, :] + pseudo
    anchor_new = anchor[mine, :] - 0.7 * (pseudo + 0.9 * momentum_new)
    own = pl.ds(pl.multiple_of(f * rows + r * quarter, quarter), quarter)
    weights[own, :] = anchor_new.astype(weights.dtype)

    def z_copy(k, h):
        ref = chunk(f, r, h)
        return remote(ref, ref, z_send.at[k, h], z_recv.at[k, h], r, 2 * ((o + k) % outer) + b)

    def source(k, parity):
        return 2 * ((o + outer - k) % outer) + parity

    def held(k, h, which):
        first, second = which % 2, which // 2
        flip, far = (first, second) if h == 0 else (second, first)
        return chunk(source(k, 1 - b if flip else b), over if far else r, h)

    def first_copy(k, h):
        ref = held(k, h, 0)
        to = (r, partner) if h == 0 else (over, f)
        return remote(ref, ref, first_send.at[k, h], first_recv.at[k, h], *to)

    def second_copy(k, h, which):
        ref = held(k, h, which)
        to = (over, f) if h == 0 else (r, partner)
        return remote(
            ref, ref, second_send.at[k, h, which], second_recv.at[k, h, which], *to
        )

    def near_copy(k, h, which):
        ref = held(k, h, which)
        return remote(
            ref, ref, near_send.at[k, h, which], near_recv.at[k, h, which], near, f
        )

    @pl.loop(1, outer)
    def _(k):
        for h in range(2):
            z_copy(k, h).start()

    total[...] = jnp.zeros_like(total)

    @pl.loop(0, outer + 3)
    def _(i):
        @pl.when(i < outer)
        def _():
            for h in range(2):
                @pl.when(i > 0)
                def _():
                    z_copy(i, h).wait_recv()

                first_copy(i, h).start()
                second_copy(i, h, 0).start()
                near_copy(i, h, 0).start()

        @pl.when((i >= 1) & (i < outer + 1))
        def _():
            for h in range(2):
                first_copy(i - 1, h).wait_recv()
                second_copy(i - 1, h, 1).start()
                near_copy(i - 1, h, 1).start()

        @pl.when((i >= 2) & (i < outer + 2))
        def _():
            for which in range(2):
                for h in range(2):
                    second_copy(i - 2, h, which).wait_recv()
                    near_copy(i - 2, h, 2 + which).start()

        @pl.when(i >= 3)
        def _():
            k = i - 3
            for h in range(2):
                for which in range(4):
                    near_copy(k, h, which).wait_recv()
            at = pl.ds(pl.multiple_of(source(k, 0) * rows, 2 * rows), 2 * rows)
            total[...] += jnp.dot(
                tokens[:, at], weights[at, :], preferred_element_type=jnp.float32
            )

    keys[...] = total[...].astype(keys.dtype)
    for m in (1, 2, 3):
        got_copy(m).wait_send()

    @pl.loop(0, outer)
    def _(k):
        for h in range(2):
            @pl.when(k > 0)
            def _():
                z_copy(k, h).wait_send()

            first_copy(k, h).wait_send()
            for which in range(2):
                second_copy(k, h, which).wait_send()
            for which in range(4):
                near_copy(k, h, which).wait_send()


def keys_of(mesh, tokens, delta, anchor, momentum):
    n = mesh.shape["fsdp"]
    outer = n // 2
    count, width = tokens.shape
    rows, kh = anchor.shape
    dma = pltpu.SemaphoreType.DMA
    return pl.pallas_call(
        functools.partial(keys_kernel, n),
        out_shape=jax.ShapeDtypeStruct((count, kh), jnp.bfloat16),
        in_specs=[VMEM] * 4,
        out_specs=VMEM,
        scratch_shapes=[
            pltpu.VMEM((3, rows // 4, kh), jnp.bfloat16),
            pltpu.VMEM((width, kh), jnp.bfloat16),
            pltpu.VMEM((count, kh), jnp.float32),
            dma((3,)), dma((3,)),
            dma((outer, 2)), dma((outer, 2)), dma((outer, 2)), dma((outer, 2)),
            dma((outer, 2, 2)), dma((outer, 2, 2)), dma((outer, 2, 4)), dma((outer, 2, 4)),
        ],
        compiler_params=pltpu.CompilerParams(
            collective_id=1, has_side_effects=True, vmem_limit_bytes=40 * 2**20
        ),
    )(tokens, delta, anchor, momentum)


def on_device(mesh, tokens, cotangent, anchor, momentum, first_moment, second_moment, inner_offset):
    grad = group_grad(mesh, tokens, cotangent)[None]
    first_new = 0.9 * first_moment + 0.1 * grad
    second_new = 0.95 * second_moment + 0.05 * grad * grad
    current = anchor[None] + inner_offset
    inner = current - 0.001 * (first_new / (jnp.sqrt(second_new) + 1e-08) + 0.1 * current)
    delta = (anchor - inner[0]).astype(jnp.bfloat16)
    keys = keys_of(mesh, tokens, delta, anchor, momentum)
    return (keys, first_new, second_new)


def solution(mesh):
    return jax.shard_map(
        functools.partial(on_device, mesh),
        mesh=mesh,
        in_specs=(
            P(("rep", "fsdp"), None),
            P(("rep", "fsdp"), None),
            P("fsdp", None),
            P("fsdp", None),
            P("rep", "fsdp", None),
            P("rep", "fsdp", None),
            P("rep", "fsdp", None),
        ),
        out_specs=(P(("rep", "fsdp"), None), P("rep", "fsdp", None), P("rep", "fsdp", None)),
        check_vma=False,
    )
```

```python
import functools
import jax
import jax.numpy as jnp
from jax import lax
from jax.experimental import pallas as pl
from jax.experimental.pallas import tpu as pltpu
from jax.sharding import PartitionSpec as P

VMEM = pl.BlockSpec(memory_space=pltpu.VMEM)


def remote(src, dst, send_sem, recv_sem, rep, fsdp):
    return pltpu.make_async_remote_copy(
        src_ref=src,
        dst_ref=dst,
        send_sem=send_sem,
        recv_sem=recv_sem,
        device_id=(rep, fsdp),
        device_id_type=pl.DeviceIdType.MESH,
    )


def greet(rep, fsdp):
    pl.semaphore_signal(
        pltpu.get_barrier_semaphore(),
        inc=1,
        device_id=(rep, fsdp),
        device_id_type=pl.DeviceIdType.MESH,
    )


def contract_rows(left, right):
    return lax.dot_general(
        left, right, (((0,), (0,)), ((), ())), preferred_element_type=jnp.float32
    )


def grad_kernel(
    n, tokens, cot, grad, tok_p, cot_p, part, recv,
    cot_send, cot_recv, tok_send, tok_recv, part_send, part_recv,
):
    outer = n // 2
    rows = grad.shape[0]
    tile = min(rows, 256)
    r, f = lax.axis_index("rep"), lax.axis_index("fsdp")
    o, b = f // 2, f % 2
    partner = 2 * o + 1 - b

    greet(r, partner)

    @pl.loop(1, outer)
    def _(k):
        greet(r, 2 * ((o + k) % outer) + b)

    pl.semaphore_wait(pltpu.get_barrier_semaphore(), outer)

    def cot_copy():
        return remote(cot, cot_p, cot_send, cot_recv, r, partner)

    def tok_copy(k):
        col = pl.multiple_of((2 * ((o + k) % outer) + 1 - b) * rows, rows)
        return remote(
            tokens.at[:, pl.ds(col, rows)], tok_p.at[k],
            tok_send.at[k], tok_recv.at[k], r, partner,
        )

    def part_copy(k):
        return remote(
            part.at[k], recv.at[k], part_send.at[k], part_recv.at[k],
            r, 2 * ((o + k) % outer) + b,
        )

    def partial(k, j):
        first = pl.multiple_of(j * tile, tile)
        col = pl.multiple_of((2 * ((o + k) % outer) + b) * rows + first, tile)
        return contract_rows(tokens[:, pl.ds(col, tile)], cot[...]) + contract_rows(
            tok_p[k, :, pl.ds(first, tile)], cot_p[...]
        )

    cot_copy().start()

    @pl.loop(1, outer)
    def _(k):
        tok_copy(k).start()

    tok_copy(0).start()
    cot_copy().wait_recv()

    @pl.loop(1, outer)
    def _(k):
        tok_copy(k).wait_recv()

        @pl.loop(0, rows // tile)
        def _(j):
            at = pl.ds(pl.multiple_of(j * tile, tile), tile)
            part[k, at, :] = partial(k, j).astype(part.dtype)

        part_copy(k).start()

    tok_copy(0).wait_recv()

    @pl.loop(0, rows // tile)
    def _(j):
        grad[pl.ds(pl.multiple_of(j * tile, tile), tile), :] = partial(0, j)

    @pl.loop(1, outer)
    def _(k):
        part_copy(k).wait_recv()

        @pl.loop(0, rows // tile)
        def _(j):
            at = pl.ds(pl.multiple_of(j * tile, tile), tile)
            grad[at, :] += recv[k, at, :].astype(jnp.float32)

    cot_copy().wait_send()
    tok_copy(0).wait_send()

    @pl.loop(1, outer)
    def _(k):
        tok_copy(k).wait_send()
        part_copy(k).wait_send()


PIECES = 4


def line_kernel(
    tokens, cot, grad, tok_p, cot_p, part, recv,
    cot_send, cot_recv, tok_send, tok_recv, part_send, part_recv,
):
    rows = grad.shape[0]
    size = rows // PIECES
    tile = min(size, 256)
    r, f = lax.axis_index("rep"), lax.axis_index("fsdp")
    o, b = f // 2, f % 2
    partner = 2 * o + 1 - b
    side = o // 2
    inner = (o + side) % 2

    def pair(q):
        return q + side * (3 - 2 * q)

    greet(r, partner)
    for k in range(1, 4):
        greet(r, 2 * ((o + k) % 4) + b)
    pl.semaphore_wait(pltpu.get_barrier_semaphore(), 4)

    def block(i):
        return (3 + inner - i) % 4

    def cot_copy():
        return remote(cot, cot_p, cot_send, cot_recv, r, partner)

    def tok_copy(i, h):
        col = pl.multiple_of((2 * pair(block(i)) + 1 - b) * rows + h * size, size)
        return remote(
            tokens.at[:, pl.ds(col, size)], tok_p.at[i, h],
            tok_send.at[i, h], tok_recv.at[i, h], r, partner,
        )

    def part_copy(i, h):
        slot = i + inner * (2, 2, 1)[i]
        to = pair(inner * block(i) + 1 - inner)
        return remote(
            part.at[i, h], recv.at[slot, h], part_send.at[i, h], part_recv.at[slot, h],
            r, 2 * to + b,
        )

    def received(slot, h):
        return remote(
            part.at[0, h], recv.at[slot, h], part_send.at[0, h], part_recv.at[slot, h],
            r, partner,
        )

    def partial(i, h, j):
        first = pl.multiple_of(j * tile, tile)
        col = pl.multiple_of((2 * pair(block(i)) + b) * rows + h * size + first, tile)
        return contract_rows(tokens[:, pl.ds(col, tile)], cot[...]) + contract_rows(
            tok_p[i, h, :, pl.ds(first, tile)], cot_p[...]
        )

    cot_copy().start()
    for i in range(4):
        for h in range(PIECES):
            tok_copy(i, h).start()
    cot_copy().wait_recv()
    for i in range(3):
        for h in range(PIECES):
            tok_copy(i, h).wait_recv()

            @pl.when((inner == 0) | (i == 0))
            def _():
                @pl.loop(0, size // tile)
                def _(j):
                    at = pl.ds(pl.multiple_of(j * tile, tile), tile)
                    part[i, h, at, :] = partial(i, h, j).astype(part.dtype)

            if i > 0:
                @pl.when(inner == 1)
                def _():
                    received(i - 1, h).wait_recv()

                    @pl.loop(0, size // tile)
                    def _(j):
                        at = pl.ds(pl.multiple_of(j * tile, tile), tile)
                        total = partial(i, h, j) + recv[i - 1, h, at, :].astype(jnp.float32)
                        part[i, h, at, :] = total.astype(part.dtype)

            part_copy(i, h).start()

    for h in range(PIECES):
        tok_copy(3, h).wait_recv()

        @pl.loop(0, size // tile)
        def _(j):
            at = pl.ds(pl.multiple_of(h * size + j * tile, tile), tile)
            grad[at, :] = partial(3, h, j)

    for h in range(PIECES):
        for slot in (2, 3):
            received(slot, h).wait_recv()

            @pl.loop(0, size // tile)
            def _(j):
                at = pl.ds(pl.multiple_of(h * size + j * tile, tile), tile)
                there = pl.ds(pl.multiple_of(j * tile, tile), tile)
                grad[at, :] += recv[slot, h, there, :].astype(jnp.float32)

    cot_copy().wait_send()
    for h in range(PIECES):
        for i in range(4):
            tok_copy(i, h).wait_send()
        for i in range(3):
            part_copy(i, h).wait_send()


def line_grad(tokens, cotangent):
    count, width = tokens.shape
    kh = cotangent.shape[1]
    rows = width // 8
    size = rows // PIECES
    dma = pltpu.SemaphoreType.DMA
    return pl.pallas_call(
        line_kernel,
        out_shape=jax.ShapeDtypeStruct((rows, kh), jnp.float32),
        in_specs=[VMEM] * 2,
        out_specs=VMEM,
        scratch_shapes=[
            pltpu.VMEM((4, PIECES, count, size), jnp.bfloat16),
            pltpu.VMEM((count, kh), jnp.bfloat16),
            pltpu.VMEM((3, PIECES, size, kh), jnp.bfloat16),
            pltpu.VMEM((4, PIECES, size, kh), jnp.bfloat16),
            dma, dma, dma((4, PIECES)), dma((4, PIECES)), dma((3, PIECES)), dma((4, PIECES)),
        ],
        compiler_params=pltpu.CompilerParams(
            collective_id=0, has_side_effects=True, vmem_limit_bytes=40 * 2**20
        ),
    )(tokens, cotangent)


def group_grad(mesh, tokens, cotangent):
    n = mesh.shape["fsdp"]
    if n == 8:
        return line_grad(tokens, cotangent)
    outer = n // 2
    count, width = tokens.shape
    kh = cotangent.shape[1]
    rows = width // n
    dma = pltpu.SemaphoreType.DMA
    return pl.pallas_call(
        functools.partial(grad_kernel, n),
        out_shape=jax.ShapeDtypeStruct((rows, kh), jnp.float32),
        in_specs=[VMEM] * 2,
        out_specs=VMEM,
        scratch_shapes=[
            pltpu.VMEM((outer, count, rows), jnp.bfloat16),
            pltpu.VMEM((count, kh), jnp.bfloat16),
            pltpu.VMEM((outer, rows, kh), jnp.bfloat16),
            pltpu.VMEM((outer, rows, kh), jnp.bfloat16),
            dma, dma, dma((outer,)), dma((outer,)), dma((outer,)), dma((outer,)),
        ],
        compiler_params=pltpu.CompilerParams(
            collective_id=0, has_side_effects=True, vmem_limit_bytes=40 * 2**20
        ),
    )(tokens, cotangent)


def keys_kernel(
    n, tokens, delta, anchor, momentum, keys, got, weights, total,
    got_send, got_recv, z_send, z_recv, first_send, first_recv,
    second_send, second_recv, near_send, near_recv,
):
    outer = n // 2
    rows = anchor.shape[0]
    quarter = rows // 4
    r, f = lax.axis_index("rep"), lax.axis_index("fsdp")
    o, b = f // 2, f % 2
    partner = 2 * o + 1 - b
    over, near = (r + 2) % 4, r + 1 - 2 * (r % 2)

    greet(r, partner)

    @pl.loop(1, outer)
    def _(k):
        greet(r, 2 * ((o + k) % outer) + b)

    for m in range(1, 4):
        greet((r + m) % 4, f)
    pl.semaphore_wait(pltpu.get_barrier_semaphore(), outer + 3)

    def quarter_of(rep):
        return pl.ds(pl.multiple_of(rep * quarter, quarter), quarter)

    def chunk(fsdp, rep, h):
        at = fsdp * rows + rep * quarter + h * (quarter // 2)
        return weights.at[pl.ds(pl.multiple_of(at, quarter // 2), quarter // 2)]

    def got_copy(m):
        to = (r + m) % 4
        return remote(
            delta.at[quarter_of(to)], got.at[m - 1],
            got_send.at[m - 1], got_recv.at[m - 1], to, f,
        )

    for m in (2, 1, 3):
        got_copy(m).start()
    mine = quarter_of(r)
    for m in (1, 2, 3):
        got_copy(m).wait_recv()
    pseudo = (
        (delta[mine, :].astype(jnp.float32) + got[0].astype(jnp.float32))
        + (got[1].astype(jnp.float32) + got[2].astype(jnp.float32))
    ) / 4
    momentum_new = 0.9 * momentum[mine, :] + pseudo
    anchor_new = anchor[mine, :] - 0.7 * (pseudo + 0.9 * momentum_new)
    own = pl.ds(pl.multiple_of(f * rows + r * quarter, quarter), quarter)
    weights[own, :] = anchor_new.astype(weights.dtype)

    def z_copy(k, h):
        ref = chunk(f, r, h)
        return remote(ref, ref, z_send.at[k, h], z_recv.at[k, h], r, 2 * ((o + k) % outer) + b)

    def source(k, parity):
        return 2 * ((o + outer - k) % outer) + parity

    def held(k, h, which):
        first, second = which % 2, which // 2
        flip, far = (first, second) if h == 0 else (second, first)
        return chunk(source(k, 1 - b if flip else b), over if far else r, h)

    def first_copy(k, h):
        ref = held(k, h, 0)
        to = (r, partner) if h == 0 else (over, f)
        return remote(ref, ref, first_send.at[k, h], first_recv.at[k, h], *to)

    def second_copy(k, h, which):
        ref = held(k, h, which)
        to = (over, f) if h == 0 else (r, partner)
        return remote(
            ref, ref, second_send.at[k, h, which], second_recv.at[k, h, which], *to
        )

    def near_copy(k, h, which):
        ref = held(k, h, which)
        return remote(
            ref, ref, near_send.at[k, h, which], near_recv.at[k, h, which], near, f
        )

    @pl.loop(1, outer)
    def _(k):
        for h in range(2):
            z_copy(k, h).start()

    total[...] = jnp.zeros_like(total)

    @pl.loop(0, outer + 3)
    def _(i):
        @pl.when(i < outer)
        def _():
            for h in range(2):
                @pl.when(i > 0)
                def _():
                    z_copy(i, h).wait_recv()

                first_copy(i, h).start()
                second_copy(i, h, 0).start()
                near_copy(i, h, 0).start()

        @pl.when((i >= 1) & (i < outer + 1))
        def _():
            for h in range(2):
                first_copy(i - 1, h).wait_recv()
                second_copy(i - 1, h, 1).start()
                near_copy(i - 1, h, 1).start()

        @pl.when((i >= 2) & (i < outer + 2))
        def _():
            for which in range(2):
                for h in range(2):
                    second_copy(i - 2, h, which).wait_recv()
                    near_copy(i - 2, h, 2 + which).start()

        @pl.when(i >= 3)
        def _():
            k = i - 3
            for h in range(2):
                for which in range(4):
                    near_copy(k, h, which).wait_recv()
            at = pl.ds(pl.multiple_of(source(k, 0) * rows, 2 * rows), 2 * rows)
            total[...] += jnp.dot(
                tokens[:, at], weights[at, :], preferred_element_type=jnp.float32
            )

    keys[...] = total[...].astype(keys.dtype)
    for m in (1, 2, 3):
        got_copy(m).wait_send()

    @pl.loop(0, outer)
    def _(k):
        for h in range(2):
            @pl.when(k > 0)
            def _():
                z_copy(k, h).wait_send()

            first_copy(k, h).wait_send()
            for which in range(2):
                second_copy(k, h, which).wait_send()
            for which in range(4):
                near_copy(k, h, which).wait_send()


def keys_of(mesh, tokens, delta, anchor, momentum):
    n = mesh.shape["fsdp"]
    outer = n // 2
    count, width = tokens.shape
    rows, kh = anchor.shape
    dma = pltpu.SemaphoreType.DMA
    return pl.pallas_call(
        functools.partial(keys_kernel, n),
        out_shape=jax.ShapeDtypeStruct((count, kh), jnp.bfloat16),
        in_specs=[VMEM] * 4,
        out_specs=VMEM,
        scratch_shapes=[
            pltpu.VMEM((3, rows // 4, kh), jnp.bfloat16),
            pltpu.VMEM((width, kh), jnp.bfloat16),
            pltpu.VMEM((count, kh), jnp.float32),
            dma((3,)), dma((3,)),
            dma((outer, 2)), dma((outer, 2)), dma((outer, 2)), dma((outer, 2)),
            dma((outer, 2, 2)), dma((outer, 2, 2)), dma((outer, 2, 4)), dma((outer, 2, 4)),
        ],
        compiler_params=pltpu.CompilerParams(
            collective_id=1, has_side_effects=True, vmem_limit_bytes=40 * 2**20
        ),
    )(tokens, delta, anchor, momentum)


def on_device(mesh, tokens, cotangent, anchor, momentum, first_moment, second_moment, inner_offset):
    grad = group_grad(mesh, tokens, cotangent)[None]
    first_new = 0.9 * first_moment + 0.1 * grad
    second_new = 0.95 * second_moment + 0.05 * grad * grad
    current = anchor[None] + inner_offset
    inner = current - 0.001 * (first_new / (jnp.sqrt(second_new) + 1e-08) + 0.1 * current)
    delta = (anchor - inner[0]).astype(jnp.bfloat16)
    keys = keys_of(mesh, tokens, delta, anchor, momentum)
    return (keys, first_new, second_new)


def solution(mesh):
    return jax.shard_map(
        functools.partial(on_device, mesh),
        mesh=mesh,
        in_specs=(
            P(("rep", "fsdp"), None),
            P(("rep", "fsdp"), None),
            P("fsdp", None),
            P("fsdp", None),
            P("rep", "fsdp", None),
            P("rep", "fsdp", None),
            P("rep", "fsdp", None),
        ),
        out_specs=(P(("rep", "fsdp"), None), P("rep", "fsdp", None), P("rep", "fsdp", None)),
        check_vma=False,
    )
```

```python
import functools
import jax
import jax.numpy as jnp
from jax import lax
from jax.experimental import pallas as pl
from jax.experimental.pallas import tpu as pltpu
from jax.sharding import PartitionSpec as P

VMEM = pl.BlockSpec(memory_space=pltpu.VMEM)


def remote(src, dst, send_sem, recv_sem, rep, fsdp):
    return pltpu.make_async_remote_copy(
        src_ref=src,
        dst_ref=dst,
        send_sem=send_sem,
        recv_sem=recv_sem,
        device_id=(rep, fsdp),
        device_id_type=pl.DeviceIdType.MESH,
    )


def greet(rep, fsdp):
    pl.semaphore_signal(
        pltpu.get_barrier_semaphore(),
        inc=1,
        device_id=(rep, fsdp),
        device_id_type=pl.DeviceIdType.MESH,
    )


def contract_rows(left, right):
    return lax.dot_general(
        left, right, (((0,), (0,)), ((), ())), preferred_element_type=jnp.float32
    )


def grad_kernel(
    n, tokens, cot, grad, tok_p, cot_p, part, recv,
    cot_send, cot_recv, tok_send, tok_recv, part_send, part_recv,
):
    outer = n // 2
    rows = grad.shape[0]
    tile = min(rows, 256)
    r, f = lax.axis_index("rep"), lax.axis_index("fsdp")
    o, b = f // 2, f % 2
    partner = 2 * o + 1 - b

    greet(r, partner)

    @pl.loop(1, outer)
    def _(k):
        greet(r, 2 * ((o + k) % outer) + b)

    pl.semaphore_wait(pltpu.get_barrier_semaphore(), outer)

    def cot_copy():
        return remote(cot, cot_p, cot_send, cot_recv, r, partner)

    def tok_copy(k):
        col = pl.multiple_of((2 * ((o + k) % outer) + 1 - b) * rows, rows)
        return remote(
            tokens.at[:, pl.ds(col, rows)], tok_p.at[k],
            tok_send.at[k], tok_recv.at[k], r, partner,
        )

    def part_copy(k):
        return remote(
            part.at[k], recv.at[k], part_send.at[k], part_recv.at[k],
            r, 2 * ((o + k) % outer) + b,
        )

    def partial(k, j):
        first = pl.multiple_of(j * tile, tile)
        col = pl.multiple_of((2 * ((o + k) % outer) + b) * rows + first, tile)
        return contract_rows(tokens[:, pl.ds(col, tile)], cot[...]) + contract_rows(
            tok_p[k, :, pl.ds(first, tile)], cot_p[...]
        )

    cot_copy().start()

    @pl.loop(1, outer)
    def _(k):
        tok_copy(k).start()

    tok_copy(0).start()
    cot_copy().wait_recv()

    @pl.loop(1, outer)
    def _(k):
        tok_copy(k).wait_recv()

        @pl.loop(0, rows // tile)
        def _(j):
            at = pl.ds(pl.multiple_of(j * tile, tile), tile)
            part[k, at, :] = partial(k, j).astype(part.dtype)

        part_copy(k).start()

    tok_copy(0).wait_recv()

    @pl.loop(0, rows // tile)
    def _(j):
        grad[pl.ds(pl.multiple_of(j * tile, tile), tile), :] = partial(0, j)

    @pl.loop(1, outer)
    def _(k):
        part_copy(k).wait_recv()

        @pl.loop(0, rows // tile)
        def _(j):
            at = pl.ds(pl.multiple_of(j * tile, tile), tile)
            grad[at, :] += recv[k, at, :].astype(jnp.float32)

    cot_copy().wait_send()
    tok_copy(0).wait_send()

    @pl.loop(1, outer)
    def _(k):
        tok_copy(k).wait_send()
        part_copy(k).wait_send()


PIECES = 8


def line_kernel(
    tokens, cot, grad, tok_p, cot_p, part, recv,
    cot_send, cot_recv, tok_send, tok_recv, part_send, part_recv,
):
    rows = grad.shape[0]
    size = rows // PIECES
    tile = min(size, 256)
    r, f = lax.axis_index("rep"), lax.axis_index("fsdp")
    o, b = f // 2, f % 2
    partner = 2 * o + 1 - b
    side = o // 2
    inner = (o + side) % 2

    def pair(q):
        return q + side * (3 - 2 * q)

    greet(r, partner)
    for k in range(1, 4):
        greet(r, 2 * ((o + k) % 4) + b)
    pl.semaphore_wait(pltpu.get_barrier_semaphore(), 4)

    def block(i):
        return (3 + inner - i) % 4

    def cot_copy():
        return remote(cot, cot_p, cot_send, cot_recv, r, partner)

    def tok_copy(i, h):
        col = pl.multiple_of((2 * pair(block(i)) + 1 - b) * rows + h * size, size)
        return remote(
            tokens.at[:, pl.ds(col, size)], tok_p.at[i, h],
            tok_send.at[i, h], tok_recv.at[i, h], r, partner,
        )

    def part_copy(i, h):
        slot = i + inner * (2, 2, 1)[i]
        to = pair(inner * block(i) + 1 - inner)
        return remote(
            part.at[i, h], recv.at[slot, h], part_send.at[i, h], part_recv.at[slot, h],
            r, 2 * to + b,
        )

    def received(slot, h):
        return remote(
            part.at[0, h], recv.at[slot, h], part_send.at[0, h], part_recv.at[slot, h],
            r, partner,
        )

    def partial(i, h, j):
        first = pl.multiple_of(j * tile, tile)
        col = pl.multiple_of((2 * pair(block(i)) + b) * rows + h * size + first, tile)
        return contract_rows(tokens[:, pl.ds(col, tile)], cot[...]) + contract_rows(
            tok_p[i, h, :, pl.ds(first, tile)], cot_p[...]
        )

    cot_copy().start()
    for i in range(4):
        for h in range(PIECES):
            tok_copy(i, h).start()
    cot_copy().wait_recv()
    for i in range(3):
        for h in range(PIECES):
            tok_copy(i, h).wait_recv()

            @pl.when((inner == 0) | (i == 0))
            def _():
                @pl.loop(0, size // tile)
                def _(j):
                    at = pl.ds(pl.multiple_of(j * tile, tile), tile)
                    part[i, h, at, :] = partial(i, h, j).astype(part.dtype)

            if i > 0:
                @pl.when(inner == 1)
                def _():
                    received(i - 1, h).wait_recv()

                    @pl.loop(0, size // tile)
                    def _(j):
                        at = pl.ds(pl.multiple_of(j * tile, tile), tile)
                        total = partial(i, h, j) + recv[i - 1, h, at, :].astype(jnp.float32)
                        part[i, h, at, :] = total.astype(part.dtype)

            part_copy(i, h).start()

    for h in range(PIECES):
        tok_copy(3, h).wait_recv()

        @pl.loop(0, size // tile)
        def _(j):
            at = pl.ds(pl.multiple_of(h * size + j * tile, tile), tile)
            grad[at, :] = partial(3, h, j)

    for h in range(PIECES):
        for slot in (2, 3):
            received(slot, h).wait_recv()

            @pl.loop(0, size // tile)
            def _(j):
                at = pl.ds(pl.multiple_of(h * size + j * tile, tile), tile)
                there = pl.ds(pl.multiple_of(j * tile, tile), tile)
                grad[at, :] += recv[slot, h, there, :].astype(jnp.float32)

    cot_copy().wait_send()
    for h in range(PIECES):
        for i in range(4):
            tok_copy(i, h).wait_send()
        for i in range(3):
            part_copy(i, h).wait_send()


def line_grad(tokens, cotangent):
    count, width = tokens.shape
    kh = cotangent.shape[1]
    rows = width // 8
    size = rows // PIECES
    dma = pltpu.SemaphoreType.DMA
    return pl.pallas_call(
        line_kernel,
        out_shape=jax.ShapeDtypeStruct((rows, kh), jnp.float32),
        in_specs=[VMEM] * 2,
        out_specs=VMEM,
        scratch_shapes=[
            pltpu.VMEM((4, PIECES, count, size), jnp.bfloat16),
            pltpu.VMEM((count, kh), jnp.bfloat16),
            pltpu.VMEM((3, PIECES, size, kh), jnp.bfloat16),
            pltpu.VMEM((4, PIECES, size, kh), jnp.bfloat16),
            dma, dma, dma((4, PIECES)), dma((4, PIECES)), dma((3, PIECES)), dma((4, PIECES)),
        ],
        compiler_params=pltpu.CompilerParams(
            collective_id=0, has_side_effects=True, vmem_limit_bytes=40 * 2**20
        ),
    )(tokens, cotangent)


def group_grad(mesh, tokens, cotangent):
    n = mesh.shape["fsdp"]
    if n == 8:
        return line_grad(tokens, cotangent)
    outer = n // 2
    count, width = tokens.shape
    kh = cotangent.shape[1]
    rows = width // n
    dma = pltpu.SemaphoreType.DMA
    return pl.pallas_call(
        functools.partial(grad_kernel, n),
        out_shape=jax.ShapeDtypeStruct((rows, kh), jnp.float32),
        in_specs=[VMEM] * 2,
        out_specs=VMEM,
        scratch_shapes=[
            pltpu.VMEM((outer, count, rows), jnp.bfloat16),
            pltpu.VMEM((count, kh), jnp.bfloat16),
            pltpu.VMEM((outer, rows, kh), jnp.bfloat16),
            pltpu.VMEM((outer, rows, kh), jnp.bfloat16),
            dma, dma, dma((outer,)), dma((outer,)), dma((outer,)), dma((outer,)),
        ],
        compiler_params=pltpu.CompilerParams(
            collective_id=0, has_side_effects=True, vmem_limit_bytes=40 * 2**20
        ),
    )(tokens, cotangent)


def keys_kernel(
    n, tokens, delta, anchor, momentum, keys, got, weights, total,
    got_send, got_recv, z_send, z_recv, first_send, first_recv,
    second_send, second_recv, near_send, near_recv,
):
    outer = n // 2
    rows = anchor.shape[0]
    quarter = rows // 4
    r, f = lax.axis_index("rep"), lax.axis_index("fsdp")
    o, b = f // 2, f % 2
    partner = 2 * o + 1 - b
    over, near = (r + 2) % 4, r + 1 - 2 * (r % 2)

    greet(r, partner)

    @pl.loop(1, outer)
    def _(k):
        greet(r, 2 * ((o + k) % outer) + b)

    for m in range(1, 4):
        greet((r + m) % 4, f)
    pl.semaphore_wait(pltpu.get_barrier_semaphore(), outer + 3)

    def quarter_of(rep):
        return pl.ds(pl.multiple_of(rep * quarter, quarter), quarter)

    def chunk(fsdp, rep, h):
        at = fsdp * rows + rep * quarter + h * (quarter // 2)
        return weights.at[pl.ds(pl.multiple_of(at, quarter // 2), quarter // 2)]

    def got_copy(m):
        to = (r + m) % 4
        return remote(
            delta.at[quarter_of(to)], got.at[m - 1],
            got_send.at[m - 1], got_recv.at[m - 1], to, f,
        )

    for m in (2, 1, 3):
        got_copy(m).start()
    mine = quarter_of(r)
    for m in (1, 2, 3):
        got_copy(m).wait_recv()
    pseudo = (
        (delta[mine, :].astype(jnp.float32) + got[0].astype(jnp.float32))
        + (got[1].astype(jnp.float32) + got[2].astype(jnp.float32))
    ) / 4
    momentum_new = 0.9 * momentum[mine, :] + pseudo
    anchor_new = anchor[mine, :] - 0.7 * (pseudo + 0.9 * momentum_new)
    own = pl.ds(pl.multiple_of(f * rows + r * quarter, quarter), quarter)
    weights[own, :] = anchor_new.astype(weights.dtype)

    def z_copy(k, h):
        ref = chunk(f, r, h)
        return remote(ref, ref, z_send.at[k, h], z_recv.at[k, h], r, 2 * ((o + k) % outer) + b)

    def source(k, parity):
        return 2 * ((o + outer - k) % outer) + parity

    def held(k, h, which):
        first, second = which % 2, which // 2
        flip, far = (first, second) if h == 0 else (second, first)
        return chunk(source(k, 1 - b if flip else b), over if far else r, h)

    def first_copy(k, h):
        ref = held(k, h, 0)
        to = (r, partner) if h == 0 else (over, f)
        return remote(ref, ref, first_send.at[k, h], first_recv.at[k, h], *to)

    def second_copy(k, h, which):
        ref = held(k, h, which)
        to = (over, f) if h == 0 else (r, partner)
        return remote(
            ref, ref, second_send.at[k, h, which], second_recv.at[k, h, which], *to
        )

    def near_copy(k, h, which):
        ref = held(k, h, which)
        return remote(
            ref, ref, near_send.at[k, h, which], near_recv.at[k, h, which], near, f
        )

    @pl.loop(1, outer)
    def _(k):
        for h in range(2):
            z_copy(k, h).start()

    total[...] = jnp.zeros_like(total)

    @pl.loop(0, outer + 3)
    def _(i):
        @pl.when(i < outer)
        def _():
            for h in range(2):
                @pl.when(i > 0)
                def _():
                    z_copy(i, h).wait_recv()

                first_copy(i, h).start()
                second_copy(i, h, 0).start()
                near_copy(i, h, 0).start()

        @pl.when((i >= 1) & (i < outer + 1))
        def _():
            for h in range(2):
                first_copy(i - 1, h).wait_recv()
                second_copy(i - 1, h, 1).start()
                near_copy(i - 1, h, 1).start()

        @pl.when((i >= 2) & (i < outer + 2))
        def _():
            for which in range(2):
                for h in range(2):
                    second_copy(i - 2, h, which).wait_recv()
                    near_copy(i - 2, h, 2 + which).start()

        @pl.when(i >= 3)
        def _():
            k = i - 3
            for h in range(2):
                for which in range(4):
                    near_copy(k, h, which).wait_recv()
            at = pl.ds(pl.multiple_of(source(k, 0) * rows, 2 * rows), 2 * rows)
            total[...] += jnp.dot(
                tokens[:, at], weights[at, :], preferred_element_type=jnp.float32
            )

    keys[...] = total[...].astype(keys.dtype)
    for m in (1, 2, 3):
        got_copy(m).wait_send()

    @pl.loop(0, outer)
    def _(k):
        for h in range(2):
            @pl.when(k > 0)
            def _():
                z_copy(k, h).wait_send()

            first_copy(k, h).wait_send()
            for which in range(2):
                second_copy(k, h, which).wait_send()
            for which in range(4):
                near_copy(k, h, which).wait_send()


def keys_of(mesh, tokens, delta, anchor, momentum):
    n = mesh.shape["fsdp"]
    outer = n // 2
    count, width = tokens.shape
    rows, kh = anchor.shape
    dma = pltpu.SemaphoreType.DMA
    return pl.pallas_call(
        functools.partial(keys_kernel, n),
        out_shape=jax.ShapeDtypeStruct((count, kh), jnp.bfloat16),
        in_specs=[VMEM] * 4,
        out_specs=VMEM,
        scratch_shapes=[
            pltpu.VMEM((3, rows // 4, kh), jnp.bfloat16),
            pltpu.VMEM((width, kh), jnp.bfloat16),
            pltpu.VMEM((count, kh), jnp.float32),
            dma((3,)), dma((3,)),
            dma((outer, 2)), dma((outer, 2)), dma((outer, 2)), dma((outer, 2)),
            dma((outer, 2, 2)), dma((outer, 2, 2)), dma((outer, 2, 4)), dma((outer, 2, 4)),
        ],
        compiler_params=pltpu.CompilerParams(
            collective_id=1, has_side_effects=True, vmem_limit_bytes=40 * 2**20
        ),
    )(tokens, delta, anchor, momentum)


def on_device(mesh, tokens, cotangent, anchor, momentum, first_moment, second_moment, inner_offset):
    grad = group_grad(mesh, tokens, cotangent)[None]
    first_new = 0.9 * first_moment + 0.1 * grad
    second_new = 0.95 * second_moment + 0.05 * grad * grad
    current = anchor[None] + inner_offset
    inner = current - 0.001 * (first_new / (jnp.sqrt(second_new) + 1e-08) + 0.1 * current)
    delta = (anchor - inner[0]).astype(jnp.bfloat16)
    keys = keys_of(mesh, tokens, delta, anchor, momentum)
    return (keys, first_new, second_new)


def solution(mesh):
    return jax.shard_map(
        functools.partial(on_device, mesh),
        mesh=mesh,
        in_specs=(
            P(("rep", "fsdp"), None),
            P(("rep", "fsdp"), None),
            P("fsdp", None),
            P("fsdp", None),
            P("rep", "fsdp", None),
            P("rep", "fsdp", None),
            P("rep", "fsdp", None),
        ),
        out_specs=(P(("rep", "fsdp"), None), P("rep", "fsdp", None), P("rep", "fsdp", None)),
        check_vma=False,
    )
```
